768 devices in a mesh: fsdp: 32 (over x, y_lo, core), rep: 24 (over z, y_hi).
Axes of the slice: x: 4, y: 8 (y_hi: 2, y_lo: 4; y = y_hi * 4 + y_lo), z: 12, core: 2. Of those that a mesh axis runs over, the one named last changes fastest.
Arguments:
- tokens: bfloat16 [4096, 24, 8192], P('fsdp', 'rep'), may hold values from -30 to 30
- norm_gain: float32 [8192], replicated, may hold values from 0.5 to 2
- w_value: bfloat16 [8192, 512], P('fsdp'), may hold values from -0.25 to 0.25
- grad_value: bfloat16 [4096, 24, 512], P('fsdp', 'rep'), may hold values from -6 to 6
Outputs:
- dw_value: float32 [8192, 512], P('fsdp')
- dtokens: bfloat16 [4096, 24, 8192], P(None, 'rep', 'fsdp')
The draws below stay inside these ranges and needn't reach their ends.
All inputs are finite; a program needn't handle non-finite values.
Results may differ from the reference program's by a relative error of at most 0.0029.
Values may be sent and summed in bfloat16 or wider, within the bound.
A program may use at most 32 MiB of HBM per device.

```python
import math
import jax
import jax.numpy as jnp
from jax import lax

D = 8192
HEAD = 128
KV_HEADS = 4
TOK_DEV = 128
COLS = 512
ROWS = 4096
GROUPS = 24
N_FSDP = 32
N_REP = 24


def draw_tokens(key, part):
    key = jax.random.fold_in(key, 11)
    base_key, column_key = jax.random.split(key, 2)
    columns = jnp.arange(D, dtype=jnp.float32) / D
    scales = 3.0 ** columns * jax.random.uniform(column_key, (D,), jnp.float32, 0.7, 1.4)
    shape = (TOK_DEV * N_FSDP, N_REP, D)
    base = jnp.clip(jax.random.normal(base_key, shape, jnp.float32), -3.5, 3.5)
    values = base * scales
    return values.astype(jnp.bfloat16)


def shard_levels(rng, dims, pieces, smallest, top_value):
    gain, own = 1.0, jax.random.fold_in(rng, 6)
    for axis_at, blocks in pieces:
        steps = jnp.exp(jax.random.uniform(jax.random.fold_in(own, axis_at), (blocks,), jnp.float32, smallest / len(pieces), top_value / len(pieces)))
        gain = gain * jnp.repeat(steps, dims[axis_at] // blocks).reshape([-1 if axis == axis_at else 1 for axis in range(len(dims))])
    return gain


def bell_draw(rng, dims, deviation, reach, cuts=(), kind=jnp.bfloat16):
    drawn = deviation * jax.random.normal(rng, dims, jnp.float32)
    if cuts:
        drawn = drawn * shard_levels(rng, dims, cuts, -0.22, 0.18)
    return jnp.clip(drawn, -reach, reach).astype(kind)


def setup_inputs(seed: int = 0) -> dict:
    seeds = jax.random.split(jax.random.key(seed), 5)
    tokens = draw_tokens(jax.random.fold_in(seeds[4], 71), 0)
    norm_gain = jnp.clip(jnp.exp(jax.random.uniform(seeds[1], (D,), jnp.float32, math.log(0.5), math.log(2.0))), 0.5, 2.0)
    w_value = bell_draw(seeds[2], (D, COLS), COLS ** -0.5, 0.25, ((0, 32),))
    grad_value = bell_draw(seeds[3], (ROWS, GROUPS, COLS), 1.0, 6.0, ((0, 32), (1, 24)))
    return dict(tokens=tokens, norm_gain=norm_gain, w_value=w_value, grad_value=grad_value)


def reference(tokens, norm_gain, w_value, grad_value):

    def one_group(index):
        values = lax.dynamic_index_in_dim(tokens, index, 1, False).astype(jnp.float32)
        grads = lax.dynamic_index_in_dim(grad_value, index, 1, False)
        scale = lax.rsqrt(lax.optimization_barrier(jnp.mean(values * values, axis=-1, keepdims=True)) + 1e-05)
        normed = (values * scale * norm_gain).astype(jnp.bfloat16)
        weight_part = lax.dot_general(normed, grads, (((0,), (0,)), ((), ())), preferred_element_type=jnp.float32)
        dnormed = lax.dot_general(grads, w_value, (((1,), (1,)), ((), ())), preferred_element_type=jnp.float32)
        inner = lax.optimization_barrier(jnp.sum(values * norm_gain * dnormed, axis=-1, keepdims=True))
        dvalues = scale * norm_gain * dnormed - values * scale * scale * scale * inner / D
        return (weight_part, dvalues.astype(jnp.bfloat16))

    def step(carry, index):
        weight_part, dvalues = one_group(index)
        return (carry + weight_part, dvalues)
    start = jnp.zeros((D, KV_HEADS * HEAD), jnp.float32)
    dw_value, stacked = lax.scan(step, start, jnp.arange(N_REP, dtype=jnp.int32))
    dtokens = jnp.transpose(stacked, (1, 0, 2))
    return (dw_value, dtokens)
```

```python
import functools
import jax
import jax.numpy as jnp
from jax import lax
from jax.experimental import pallas as pl
from jax.experimental.pallas import tpu as pltpu
from jax.sharding import PartitionSpec as P

MESH = pl.DeviceIdType.MESH
NX, NY, NC = 4, 4, 2
NZ, NH = 12, 2
NF, NR = NX * NY * NC, NZ * NH
T = 128
F = 128
C = 512
D = 2 * F * NF
OWN = 8
PR = F // OWN
f32, bf16 = jnp.float32, jnp.bfloat16


def kernel(tok, gain, w, grd, dw, dt, vtok, tbuf, gbuf, dn, pacc, sc, colc, rows, acc, rsb, psum, prb, agb, dtb, dwb,
           lsem, gsend, grecv, tsend, trecv, ssem, rsem):
    me, rep = lax.axis_index("fsdp"), lax.axis_index("rep")
    x, y, c = me // (NY * NC), (me // NC) % NY, me % NC
    z, h = rep // NH, rep % NH

    def slot_of(x, y, c):
        return c * (NX * NY) + x * NY + y

    def slot_at(k):
        s = (me + NF - k) % NF
        return slot_of(s // (NY * NC), (s // NC) % NY, s % NC)

    mine = slot_of(x, y, c)
    owner = z % 3 < 2
    piece = (z // 3) * 2 + z % 3

    def local(src, dst, sem):
        return pltpu.make_async_copy(src, dst, sem)

    def to(src, dst, ss, rs, f, r):
        return pltpu.make_async_remote_copy(src_ref=src, dst_ref=dst, send_sem=ss, recv_sem=rs, device_id=(f, r), device_id_type=MESH)

    def wait(ref, sem):
        pltpu.make_async_copy(ref, ref, sem).wait()

    bar = pltpu.get_barrier_semaphore()

    def greet_f(k, _):
        pl.semaphore_signal(bar, inc=1, device_id=((me + k) % NF, rep), device_id_type=MESH)
        return 0

    def greet_z(k, _):
        pl.semaphore_signal(bar, inc=1, device_id=(me, (z + k) % NZ * NH + h), device_id_type=MESH)
        return 0

    lax.fori_loop(1, NF, greet_f, 0)
    lax.fori_loop(1, NZ, greet_z, 0)
    pl.semaphore_signal(bar, inc=1, device_id=(me, z * NH + 1 - h), device_id_type=MESH)

    load = local(tok, vtok, lsem.at[0])
    load.start()
    own_g = local(grd, gbuf.at[mine], lsem.at[1])
    own_g.start()
    own_t = [local(tok.at[:, pl.ds(pl.multiple_of((me * 2 + i) * F, F), F)], tbuf.at[i * NF + mine], trecv.at[i * NF + mine]) for i in range(2)]
    for cp in own_t:
        cp.start()
    load.wait()

    def square(i, a):
        v = vtok[:, pl.ds(pl.multiple_of(i * F, F), F)].astype(f32)
        return a + v * v

    total = lax.fori_loop(0, D // F, square, jnp.zeros((T, F), f32), unroll=4)
    srow = lax.rsqrt(jnp.sum(total.T, axis=0, keepdims=True) / D + 1e-05)
    sc[mine] = srow
    pl.semaphore_wait(bar, NF - 1 + NZ)

    own_g.wait()
    for j in range(1, NY):
        to(gbuf.at[mine], gbuf.at[mine], gsend.at[j - 1], grecv.at[mine], x * (NY * NC) + (y + j) % NY * NC + c, rep).start()
    for j in range(1, NX):
        to(gbuf.at[mine], gbuf.at[mine], gsend.at[NY + j - 2], grecv.at[mine], (x + j) % NX * (NY * NC) + y * NC + c, rep).start()
    to(gbuf.at[mine], gbuf.at[mine], gsend.at[NY + NX - 2], grecv.at[mine], me + 1 - 2 * c, rep).start()
    n_g = NY + NX - 1

    def send_scale(k, _):
        to(sc.at[mine], sc.at[mine], ssem.at[0], rsem.at[0], (me + k) % NF, rep).start()
        return 0

    lax.fori_loop(1, NF, send_scale, 0)

    def send_tokens(i):
        def body(k, _):
            d = (me + k) % NF
            to(tok.at[:, pl.ds(pl.multiple_of((d * 2 + i) * F, F), F)], tbuf.at[i * NF + mine], tsend.at[i], trecv.at[i * NF + mine], d, rep).start()
            return 0
        lax.fori_loop(1, NF, body, 0)

    send_tokens(0)
    for i in range(1, NY):
        s = slot_of(x, (y + i) % NY, c)
        wait(gbuf.at[s], grecv.at[s])
        for j in range(1, NX):
            to(gbuf.at[s], gbuf.at[s], gsend.at[n_g], grecv.at[s], (x + j) % NX * (NY * NC) + y * NC + c, rep).start()
            n_g += 1
        to(gbuf.at[s], gbuf.at[s], gsend.at[n_g], grecv.at[s], me + 1 - 2 * c, rep).start()
        n_g += 1
    send_tokens(1)

    def dnormed(s):
        dn[s] = lax.dot_general(gbuf[s], w[...], (((1,), (1,)), ((), ())), preferred_element_type=f32)

    for i in range(NY):
        for j in range(1, NX):
            s = slot_of((x + j) % NX, (y + i) % NY, c)
            wait(gbuf.at[s], grecv.at[s])
            to(gbuf.at[s], gbuf.at[s], gsend.at[n_g], grecv.at[s], me + 1 - 2 * c, rep).start()
            n_g += 1

    def near(i, _):
        dnormed(c * (NX * NY) + i)
        return 0

    def far(i, _):
        s = (1 - c) * (NX * NY) + i
        wait(gbuf.at[s], grecv.at[s])
        dnormed(s)
        return 0

    lax.fori_loop(0, NX * NY, near, 0)
    lax.fori_loop(0, NX * NY, far, 0)

    def columns(ref):
        flat = jnp.concatenate([ref[s] for s in range(NF)] + [jnp.zeros((T - NF, T), f32)], axis=0).T
        return flat

    wait(sc.at[pl.ds(0, NF - 1)], rsem.at[0])
    flat = columns(sc)
    for s in range(NF):
        colc[0, s] = flat[:, s:s + 1]

    def gains(i):
        return gain[pl.ds(me * 2 + i, 1), :]

    def block(i, k):
        s = slot_at(k)
        wait(tbuf.at[i * NF + s], trecv.at[i * NF + s])
        v = tbuf[i * NF + s].astype(f32)
        normed = (v * colc[0, s] * gains(i)).astype(bf16)
        part = lax.dot_general(normed, gbuf[s], (((0,), (0,)), ((), ())), preferred_element_type=f32)
        acc[i] += part
        p = v * gains(i) * dn[s, :, i * F:(i + 1) * F]
        return s, p

    acc[...] = jnp.zeros_like(acc)

    def first(k, _):
        s, p = block(0, k)
        pacc[s] = p
        return 0

    lax.fori_loop(0, NF, first, 0)

    def dw_scatter(i):
        for p in range(OWN):
            zo = p // 2 * 3 + p % 2

            @pl.when(z != zo)
            def _():
                to(acc.at[i, pl.ds(p * PR, PR)], rsb.at[i, z], ssem.at[3 + i], rsem.at[3 + i], me, zo * NH + h).start()

    def dw_pair(i):
        @pl.when(owner)
        def _():
            wait(rsb.at[i, pl.ds(0, NZ - 1)], rsem.at[3 + i])
            rsb[i, z] = acc[i, pl.ds(pl.multiple_of(piece * PR, PR), PR)]
            psum[i] = functools.reduce(jnp.add, [rsb[i, j] for j in range(NZ)])
            to(psum.at[i], prb.at[i], ssem.at[5 + i], rsem.at[5 + i], me, z * NH + 1 - h).start()

    def dw_gather(i):
        @pl.when(owner)
        def _():
            wait(prb.at[i], rsem.at[5 + i])
            agb[i, piece] = (psum[i] + prb[i]).astype(bf16)

            def body(k, _):
                to(agb.at[i, piece], agb.at[i, piece], ssem.at[7 + i], rsem.at[7 + i], me, (z + k) % NZ * NH + h).start()
                return 0
            lax.fori_loop(1, NZ, body, 0)

    def dw_finish(i):
        @pl.when(owner)
        def _():
            wait(agb.at[i, pl.ds(0, OWN - 1)], rsem.at[7 + i])

        @pl.when(jnp.logical_not(owner))
        def _():
            wait(agb.at[i, pl.ds(0, OWN)], rsem.at[7 + i])
        for p in range(OWN):
            dwb[pl.ds(i * F + p * PR, PR), :] = agb[i, p].astype(f32)
        local(dwb.at[pl.ds(i * F, F)], dw.at[pl.ds(i * F, F)], lsem.at[2 + i]).start()

    def second(k, _):
        s, p = block(1, k)
        rows[0, s] = jnp.sum((p + pacc[s]).T, axis=0, keepdims=True)

        @pl.when(k > 0)
        def _():
            to(rows.at[0, s], rows.at[1, mine], ssem.at[1], rsem.at[1], (me + NF - k) % NF, rep).start()
        return 0

    dw_scatter(0)
    lax.fori_loop(0, NF // 2, second, 0)
    dw_pair(0)
    lax.fori_loop(NF // 2, NF * 3 // 4, second, 0)
    dw_gather(0)
    lax.fori_loop(NF * 3 // 4, NF, second, 0)
    dw_scatter(1)

    wait(rows.at[1, pl.ds(0, NF - 1)], rsem.at[1])
    rows[1, mine] = rows[0, mine]
    inner = functools.reduce(jnp.add, [rows[1, s] for s in range(NF)])
    srow = sc[mine]
    rows[2, mine] = srow * srow * srow * inner / D

    def send_coef(k, _):
        to(rows.at[2, mine], rows.at[2, mine], ssem.at[2], rsem.at[2], (me + k) % NF, rep).start()
        return 0

    lax.fori_loop(1, NF, send_coef, 0)
    dw_finish(0)
    dw_pair(1)
    wait(rows.at[2, pl.ds(0, NF - 1)], rsem.at[2])
    flat = columns(rows.at[2])
    for s in range(NF):
        colc[1, s] = flat[:, s:s + 1]

    def finish(k, _):
        xs = k // (NY * NC)
        s = slot_of(xs, (k // NC) % NY, k % NC)
        for i in range(2):
            a = colc[0, s] * gains(i) * dn[s, :, i * F:(i + 1) * F]
            dtb[k, :, i * F:(i + 1) * F] = (a - tbuf[i * NF + s].astype(f32) * colc[1, s]).astype(bf16)
        local(dtb.at[k], dt.at[pl.ds(pl.multiple_of(k * T, T), T)], lsem.at[4]).start()
        return 0

    lax.fori_loop(0, NF, finish, 0)
    dw_gather(1)
    dw_finish(1)

    for i in range(2):
        wait(tbuf.at[pl.ds(0, NF - 1)], tsend.at[i])
        wait(dwb.at[pl.ds(i * F, F)], lsem.at[2 + i])

        @pl.when(owner)
        def _():
            wait(acc.at[i, pl.ds(0, F - PR)], ssem.at[3 + i])
            wait(psum.at[i], ssem.at[5 + i])
            wait(agb.at[pl.ds(0, 1)].at[0, pl.ds(0, OWN)], ssem.at[7 + i])
            wait(agb.at[0, pl.ds(0, NZ - 1 - OWN)], ssem.at[7 + i])

        @pl.when(jnp.logical_not(owner))
        def _():
            wait(acc.at[i], ssem.at[3 + i])
    for i in range(3):
        wait(rows.at[0, pl.ds(0, NF - 1)], ssem.at[i])
    for j in range(n_g):
        wait(gbuf.at[0], gsend.at[j])
    wait(dtb, lsem.at[4])


def body(tokens, norm_gain, w_value, grad_value):
    anyspace, vmem = pl.BlockSpec(memory_space=pl.ANY), pl.BlockSpec(memory_space=pltpu.VMEM)
    dma = pltpu.SemaphoreType.DMA
    dw, dt = pl.pallas_call(
        kernel,
        out_shape=(jax.ShapeDtypeStruct((2 * F, C), f32), jax.ShapeDtypeStruct((NF * T, 2 * F), bf16)),
        in_specs=[anyspace, vmem, vmem, anyspace],
        out_specs=(anyspace, anyspace),
        scratch_shapes=[
            pltpu.VMEM((T, D), bf16),
            pltpu.VMEM((2 * NF, T, F), bf16),
            pltpu.VMEM((NF, T, C), bf16),
            pltpu.VMEM((NF, T, 2 * F), f32),
            pltpu.VMEM((NF, T, F), f32),
            pltpu.VMEM((NF, 1, T), f32),
            pltpu.VMEM((2, NF, T, 1), f32),
            pltpu.VMEM((3, NF, 1, T), f32),
            pltpu.VMEM((2, F, C), f32),
            pltpu.VMEM((2, NZ, PR, C), f32),
            pltpu.VMEM((2, PR, C), f32),
            pltpu.VMEM((2, PR, C), f32),
            pltpu.VMEM((2, OWN, PR, C), bf16),
            pltpu.VMEM((NF, T, 2 * F), bf16),
            pltpu.VMEM((2 * F, C), f32),
            dma((5,)), dma((48,)), dma((NF,)), dma((2,)), dma((2 * NF,)), dma((9,)), dma((9,)),
        ],
        compiler_params=pltpu.CompilerParams(collective_id=0, has_side_effects=True, vmem_limit_bytes=48 << 20),
    )(tokens.reshape(T, D), norm_gain.reshape(2 * NF, F), w_value, grad_value.reshape(T, C))
    return dw, dt.reshape(NF * T, 1, 2 * F)


def solution(mesh):
    assert mesh.shape["fsdp"] == NF and mesh.shape["rep"] == NR
    in_specs = (P("fsdp", "rep", None), P(), P("fsdp", None), P("fsdp", "rep", None))
    out_specs = (P("fsdp", None), P(None, "rep", "fsdp"))
    return jax.shard_map(body, mesh=mesh, in_specs=in_specs, out_specs=out_specs, check_vma=False)
```

```python
import functools
import jax
import jax.numpy as jnp
from jax import lax
from jax.experimental import pallas as pl
from jax.experimental.pallas import tpu as pltpu
from jax.sharding import PartitionSpec as P

MESH = pl.DeviceIdType.MESH
NX, NY, NC = 4, 4, 2
NZ, NH = 12, 2
NF, NR = NX * NY * NC, NZ * NH
T = 128
F = 128
C = 512
D = 2 * F * NF
OWN = 8
PR = F // OWN
L = NY
NG = NF // L
f32, bf16 = jnp.float32, jnp.bfloat16


def kernel(tok, gain, w, grd, dw, dt, vtok, tbuf, gbuf, dn, pacc, sc, colc, rows, acc, accb, rsf, rsb, psum, prb, agb, dtb, dwb,
           lsem, gsend, csend, grecv, tsend, trecv, ssem, rsem):
    me, rep = lax.axis_index("fsdp"), lax.axis_index("rep")
    x, y, c = me // (NY * NC), (me // NC) % NY, me % NC
    z, h = rep // NH, rep % NH

    def slot_of(x, y, c):
        return c * (NX * NY) + x * NY + y

    def shift(q):
        r = q % NX
        return r + r // 2 * (1 - 2 * (r % 2)), q // NX

    def base_of(q):
        dx, dc = shift(q)
        return slot_of((x + NX - dx) % NX, 0, (c + dc) % NC)

    mine = slot_of(x, y, c)
    owner = z % 3 < 2
    piece = (z // 3) * 2 + z % 3

    def local(src, dst, sem):
        return pltpu.make_async_copy(src, dst, sem)

    def to(src, dst, ss, rs, f, r):
        return pltpu.make_async_remote_copy(src_ref=src, dst_ref=dst, send_sem=ss, recv_sem=rs, device_id=(f, r), device_id_type=MESH)

    def wait(ref, sem):
        pltpu.make_async_copy(ref, ref, sem).wait()

    bar = pltpu.get_barrier_semaphore()

    def greet_f(k, _):
        pl.semaphore_signal(bar, inc=1, device_id=((me + k) % NF, rep), device_id_type=MESH)
        return 0

    def greet_z(k, _):
        pl.semaphore_signal(bar, inc=1, device_id=(me, (z + k) % NZ * NH + h), device_id_type=MESH)
        return 0

    lax.fori_loop(1, NF, greet_f, 0)
    lax.fori_loop(1, NZ, greet_z, 0)
    pl.semaphore_signal(bar, inc=1, device_id=(me, z * NH + 1 - h), device_id_type=MESH)

    load = local(tok, vtok, lsem.at[0])
    load.start()
    own_g = local(grd, gbuf.at[mine], lsem.at[1])
    own_g.start()
    own_t = [local(tok.at[:, pl.ds(pl.multiple_of((me * 2 + i) * F, F), F)], tbuf.at[i * NF + mine], trecv.at[i * NF + mine]) for i in range(2)]
    for cp in own_t:
        cp.start()
    load.wait()

    def square(i, a):
        v = vtok[:, pl.ds(pl.multiple_of(i * F, F), F)].astype(f32)
        return a + v * v

    total = lax.fori_loop(0, D // F, square, jnp.zeros((T, F), f32), unroll=4)
    srow = lax.rsqrt(jnp.sum(total.T, axis=0, keepdims=True) / D + 1e-05)
    sc[mine] = srow
    pl.semaphore_wait(bar, NF - 1 + NZ)

    def spread(yy):
        s = slot_of(x, yy, c)
        src = gbuf.at[s]

        @pl.when(jnp.logical_and(yy <= y, y < NY - 1))
        def _():
            to(src, src, gsend.at[yy * 8], grecv.at[s], me + NC, rep).start()

        @pl.when(jnp.logical_and(yy >= y, y > 0))
        def _():
            to(src, src, gsend.at[yy * 8 + 1], grecv.at[s], me - NC, rep).start()
        for j in range(1, NX):
            to(src, src, gsend.at[yy * 8 + 1 + j], grecv.at[s], (x + j) % NX * (NY * NC) + y * NC + c, rep).start()
        to(src, src, gsend.at[yy * 8 + 5], grecv.at[s], me + 1 - 2 * c, rep).start()

    def send_tokens(i, q0, q1):
        def body(k, _):
            dx, dc = shift(k // L)
            d = slot_dev((x + dx) % NX, (y + k) % NY, (c + dc) % NC)
            to(tok.at[:, pl.ds(pl.multiple_of((d * 2 + i) * F, F), F)], tbuf.at[i * NF + mine], tsend.at[i], trecv.at[i * NF + mine], d, rep).start()
            return 0
        lax.fori_loop(max(q0 * L, 1), q1 * L, body, 0)

    def slot_dev(x, y, c):
        return x * (NY * NC) + y * NC + c

    own_g.wait()
    spread(y)

    def send_scale(k, _):
        to(sc.at[mine], sc.at[mine], ssem.at[0], rsem.at[0], (me + k) % NF, rep).start()
        return 0

    lax.fori_loop(1, NF, send_scale, 0)
    send_tokens(0, 0, NX)
    for t in range(1, NY):
        @pl.when(y >= t)
        def _():
            s = slot_of(x, y - t, c)
            wait(gbuf.at[s], grecv.at[s])
            spread(y - t)

        @pl.when(y + t < NY)
        def _():
            s = slot_of(x, y + t, c)
            wait(gbuf.at[s], grecv.at[s])
            spread(y + t)
    send_tokens(0, NX, NG)

    def take_grads(q):
        s0 = base_of(q)

        def body(j, _):
            s = s0 + j
            wait(gbuf.at[s], grecv.at[s])

            @pl.when(q < NX)
            def _():
                to(gbuf.at[s], gbuf.at[s], csend.at[s % (NX * NY)], grecv.at[s], me + 1 - 2 * c, rep).start()
            return 0
        lax.fori_loop(0, L, body, 0)

    def dnormed(q):
        s0 = base_of(q)
        r = lax.dot_general(gbuf[pl.ds(s0, L)].reshape(L * T, C), w[...], (((1,), (1,)), ((), ())), preferred_element_type=f32)
        dn[pl.ds(s0, L)] = r.reshape(L, T, 2 * F)

    def columns(ref):
        flat = jnp.concatenate([ref[s] for s in range(NF)] + [jnp.zeros((T - NF, T), f32)], axis=0).T
        return flat

    def gains(i):
        return gain[pl.ds(me * 2 + i, 1), :]

    def block(i, q):
        s0 = base_of(q)

        def arrive(j, _):
            wait(tbuf.at[i * NF + s0 + j], trecv.at[i * NF + s0 + j])
            return 0
        lax.fori_loop(0, L, arrive, 0)
        v = tbuf[pl.ds(i * NF + s0, L)].astype(f32)
        normed = (v * colc[0, pl.ds(s0, L)] * gains(i)).astype(bf16).reshape(L * T, F)
        part = lax.dot_general(normed, gbuf[pl.ds(s0, L)].reshape(L * T, C), (((0,), (0,)), ((), ())), preferred_element_type=f32)
        acc[i] += part
        return s0, v * gains(i) * dn[pl.ds(s0, L), :, i * F:(i + 1) * F]

    def first(q, _):
        @pl.when(q > 0)
        def _():
            take_grads(q)
        dnormed(q)
        s0, p = block(0, q)
        pacc[pl.ds(s0, L)] = p
        return 0

    acc[...] = jnp.zeros_like(acc)
    wait(sc.at[pl.ds(0, NF - 1)], rsem.at[0])
    flat = columns(sc)
    for s in range(NF):
        colc[0, s] = flat[:, s:s + 1]
    send_tokens(1, 0, NX)
    lax.fori_loop(0, NX, first, 0)
    send_tokens(1, NX, NG)
    lax.fori_loop(NX, NG, first, 0)

    def dw_scatter(i):
        if i:
            accb[...] = acc[i].astype(bf16)
        src, dst = (accb, rsb) if i else (acc.at[0], rsf)
        for p in range(OWN):
            zo = p // 2 * 3 + p % 2

            @pl.when(z != zo)
            def _():
                to(src.at[pl.ds(p * PR, PR)], dst.at[z], ssem.at[3 + i], rsem.at[3 + i], me, zo * NH + h).start()

    def dw_pair(i):
        dst = rsb if i else rsf

        @pl.when(owner)
        def _():
            wait(dst.at[pl.ds(0, NZ - 1)], rsem.at[3 + i])
            own = acc[i, pl.ds(pl.multiple_of(piece * PR, PR), PR)]
            dst[z] = jnp.zeros((PR, C), dst.dtype)
            psum[i] = functools.reduce(jnp.add, [own] + [dst[j].astype(f32) for j in range(NZ)])
            to(psum.at[i], prb.at[i], ssem.at[5 + i], rsem.at[5 + i], me, z * NH + 1 - h).start()

    def dw_gather(i):
        @pl.when(owner)
        def _():
            wait(prb.at[i], rsem.at[5 + i])
            agb[i, piece] = (psum[i] + prb[i]).astype(bf16)

            def body(k, _):
                to(agb.at[i, piece], agb.at[i, piece], ssem.at[7 + i], rsem.at[7 + i], me, (z + k) % NZ * NH + h).start()
                return 0
            lax.fori_loop(1, NZ, body, 0)

    def dw_finish(i):
        @pl.when(owner)
        def _():
            wait(agb.at[i, pl.ds(0, OWN - 1)], rsem.at[7 + i])

        @pl.when(jnp.logical_not(owner))
        def _():
            wait(agb.at[i, pl.ds(0, OWN)], rsem.at[7 + i])
        for p in range(OWN):
            dwb[pl.ds(i * F + p * PR, PR), :] = agb[i, p].astype(f32)
        local(dwb.at[pl.ds(i * F, F)], dw.at[pl.ds(i * F, F)], lsem.at[2 + i]).start()

    def second(q, _):
        s0, p = block(1, q)
        dx, dc = shift(q)
        p = p + pacc[pl.ds(s0, L)]
        for j in range(L):
            rows[0, s0 + j] = jnp.sum(p[j].T, axis=0, keepdims=True)
            d = slot_dev((x + NX - dx) % NX, j, (c + dc) % NC)

            @pl.when(d != me)
            def _():
                to(rows.at[0, s0 + j], rows.at[1, mine], ssem.at[1], rsem.at[1], d, rep).start()
        return 0

    dw_scatter(0)
    lax.fori_loop(0, NG // 2, second, 0)
    dw_pair(0)
    lax.fori_loop(NG // 2, NG * 3 // 4, second, 0)
    dw_gather(0)
    lax.fori_loop(NG * 3 // 4, NG, second, 0)
    dw_scatter(1)

    wait(rows.at[1, pl.ds(0, NF - 1)], rsem.at[1])
    rows[1, mine] = rows[0, mine]
    inner = functools.reduce(jnp.add, [rows[1, s] for s in range(NF)])
    srow = sc[mine]
    rows[2, mine] = srow * srow * srow * inner / D

    def send_coef(k, _):
        to(rows.at[2, mine], rows.at[2, mine], ssem.at[2], rsem.at[2], (me + k) % NF, rep).start()
        return 0

    lax.fori_loop(1, NF, send_coef, 0)
    dw_finish(0)
    dw_pair(1)
    wait(rows.at[2, pl.ds(0, NF - 1)], rsem.at[2])
    flat = columns(rows.at[2])
    for s in range(NF):
        colc[1, s] = flat[:, s:s + 1]

    def finish(k, _):
        xs = k // (NY * NC)
        s = slot_of(xs, (k // NC) % NY, k % NC)
        for i in range(2):
            a = colc[0, s] * gains(i) * dn[s, :, i * F:(i + 1) * F]
            dtb[k, :, i * F:(i + 1) * F] = (a - tbuf[i * NF + s].astype(f32) * colc[1, s]).astype(bf16)
        local(dtb.at[k], dt.at[pl.ds(pl.multiple_of(k * T, T), T)], lsem.at[4]).start()
        return 0

    lax.fori_loop(0, NF, finish, 0)
    dw_gather(1)
    dw_finish(1)

    for i in range(2):
        wait(tbuf.at[pl.ds(0, NF - 1)], tsend.at[i])
        wait(dwb.at[pl.ds(i * F, F)], lsem.at[2 + i])

        @pl.when(owner)
        def _():
            wait((accb if i else acc.at[0]).at[pl.ds(0, F - PR)], ssem.at[3 + i])
            wait(psum.at[i], ssem.at[5 + i])
            wait(agb.at[pl.ds(0, 1)].at[0, pl.ds(0, OWN)], ssem.at[7 + i])
            wait(agb.at[0, pl.ds(0, NZ - 1 - OWN)], ssem.at[7 + i])

        @pl.when(jnp.logical_not(owner))
        def _():
            wait(accb if i else acc.at[0], ssem.at[3 + i])
    for i in range(3):
        wait(rows.at[0, pl.ds(0, NF - 1)], ssem.at[i])
    for yy in range(NY):
        @pl.when(jnp.logical_and(yy <= y, y < NY - 1))
        def _():
            wait(gbuf.at[0], gsend.at[yy * 8])

        @pl.when(jnp.logical_and(yy >= y, y > 0))
        def _():
            wait(gbuf.at[0], gsend.at[yy * 8 + 1])
        for j in range(2, 6):
            wait(gbuf.at[0], gsend.at[yy * 8 + j])
    for q in range(1, NX):
        for j in range(L):
            wait(gbuf.at[0], csend.at[base_of(q) % (NX * NY) + j])
    wait(dtb, lsem.at[4])


def body(tokens, norm_gain, w_value, grad_value):
    hbm, anyspace, vmem = pl.BlockSpec(memory_space=pltpu.HBM), pl.BlockSpec(memory_space=pl.ANY), pl.BlockSpec(memory_space=pltpu.VMEM)
    dma = pltpu.SemaphoreType.DMA
    dw, dt = pl.pallas_call(
        kernel,
        out_shape=(jax.ShapeDtypeStruct((2 * F, C), f32), jax.ShapeDtypeStruct((NF * T, 2 * F), bf16)),
        in_specs=[hbm, vmem, vmem, hbm],
        out_specs=(anyspace, anyspace),
        scratch_shapes=[
            pltpu.VMEM((T, D), bf16),
            pltpu.VMEM((2 * NF, T, F), bf16),
            pltpu.VMEM((NF, T, C), bf16),
            pltpu.VMEM((NF, T, 2 * F), f32),
            pltpu.VMEM((NF, T, F), f32),
            pltpu.VMEM((NF, 1, T), f32),
            pltpu.VMEM((2, NF, T, 1), f32),
            pltpu.VMEM((3, NF, 1, T), f32),
            pltpu.VMEM((2, F, C), f32),
            pltpu.VMEM((F, C), bf16),
            pltpu.VMEM((NZ, PR, C), f32),
            pltpu.VMEM((NZ, PR, C), bf16),
            pltpu.VMEM((2, PR, C), f32),
            pltpu.VMEM((2, PR, C), f32),
            pltpu.VMEM((2, OWN, PR, C), bf16),
            pltpu.VMEM((NF, T, 2 * F), bf16),
            pltpu.VMEM((2 * F, C), f32),
            dma((5,)), dma((NY * 8,)), dma((NX * NY,)), dma((NF,)), dma((2,)), dma((2 * NF,)), dma((9,)), dma((9,)),
        ],
        compiler_params=pltpu.CompilerParams(collective_id=0, has_side_effects=True, vmem_limit_bytes=48 << 20),
    )(tokens.reshape(T, D), norm_gain.reshape(2 * NF, F), w_value, grad_value.reshape(T, C))
    return dw, dt.reshape(NF * T, 1, 2 * F)


def solution(mesh):
    assert mesh.shape["fsdp"] == NF and mesh.shape["rep"] == NR
    in_specs = (P("fsdp", "rep", None), P(), P("fsdp", None), P("fsdp", "rep", None))
    out_specs = (P("fsdp", None), P(None, "rep", "fsdp"))
    return jax.shard_map(body, mesh=mesh, in_specs=in_specs, out_specs=out_specs, check_vma=False)
```

```python
import functools
import jax
import jax.numpy as jnp
from jax import lax
from jax.experimental import pallas as pl
from jax.experimental.pallas import tpu as pltpu
from jax.sharding import PartitionSpec as P

MESH = pl.DeviceIdType.MESH
NX, NY, NC = 4, 4, 2
NZ, NH = 12, 2
NF, NR = NX * NY * NC, NZ * NH
T = 128
F = 128
C = 512
D = 2 * F * NF
OWN = 8
PR = F // OWN
L = NY
NG = NF // L
f32, bf16 = jnp.float32, jnp.bfloat16


def kernel(tok, gain, w, grd, dw, dt, vtok, tbuf, gbuf, dn, pacc, sc, colc, rows, acc, accb, rsf, rsb, psum, prb, agb, dtb, dwb,
           lsem, gsend, csend, grecv, tsend, trecv, ssem, rsem):
    me, rep = lax.axis_index("fsdp"), lax.axis_index("rep")
    x, y, c = me // (NY * NC), (me // NC) % NY, me % NC
    z, h = rep // NH, rep % NH

    def slot_of(x, y, c):
        return c * (NX * NY) + x * NY + y

    def shift(q):
        r = q % NX
        return r + r // 2 * (1 - 2 * (r % 2)), q // NX

    def base_of(q):
        dx, dc = shift(q)
        return slot_of((x + NX - dx) % NX, 0, (c + dc) % NC)

    mine = slot_of(x, y, c)
    owner = z % 3 < 2
    piece = (z // 3) * 2 + z % 3

    def local(src, dst, sem):
        return pltpu.make_async_copy(src, dst, sem)

    def to(src, dst, ss, rs, f, r):
        return pltpu.make_async_remote_copy(src_ref=src, dst_ref=dst, send_sem=ss, recv_sem=rs, device_id=(f, r), device_id_type=MESH)

    def wait(ref, sem):
        pltpu.make_async_copy(ref, ref, sem).wait()

    bar = pltpu.get_barrier_semaphore()

    def greet_f(k, _):
        pl.semaphore_signal(bar, inc=1, device_id=((me + k) % NF, rep), device_id_type=MESH)
        return 0

    def greet_z(k, _):
        pl.semaphore_signal(bar, inc=1, device_id=(me, (z + k) % NZ * NH + h), device_id_type=MESH)
        return 0

    lax.fori_loop(1, NF, greet_f, 0)
    lax.fori_loop(1, NZ, greet_z, 0)
    pl.semaphore_signal(bar, inc=1, device_id=(me, z * NH + 1 - h), device_id_type=MESH)

    load = local(tok, vtok, lsem.at[0])
    load.start()
    own_g = local(grd, gbuf.at[mine], lsem.at[1])
    own_g.start()
    own_t = [local(tok.at[:, pl.ds(pl.multiple_of((me * 2 + i) * F, F), F)], tbuf.at[i * NF + mine], trecv.at[i * NF + mine]) for i in range(2)]
    for cp in own_t:
        cp.start()
    load.wait()

    def square(i, a):
        v = vtok[:, pl.ds(pl.multiple_of(i * F, F), F)].astype(f32)
        return a + v * v

    total = lax.fori_loop(0, D // F, square, jnp.zeros((T, F), f32), unroll=4)
    srow = lax.rsqrt(jnp.sum(total.T, axis=0, keepdims=True) / D + 1e-05)
    sc[mine] = srow
    pl.semaphore_wait(bar, NF - 1 + NZ)

    def spread(yy):
        s = slot_of(x, yy, c)
        src = gbuf.at[s]

        @pl.when(jnp.logical_and(yy <= y, y < NY - 1))
        def _():
            to(src, src, gsend.at[yy * 8], grecv.at[s], me + NC, rep).start()

        @pl.when(jnp.logical_and(yy >= y, y > 0))
        def _():
            to(src, src, gsend.at[yy * 8 + 1], grecv.at[s], me - NC, rep).start()
        for j in range(1, NX):
            to(src, src, gsend.at[yy * 8 + 1 + j], grecv.at[s], (x + j) % NX * (NY * NC) + y * NC + c, rep).start()
        to(src, src, gsend.at[yy * 8 + 5], grecv.at[s], me + 1 - 2 * c, rep).start()

    def send_tokens(i, q0, q1):
        def body(k, _):
            dx, dc = shift(k // L)
            d = slot_dev((x + dx) % NX, (y + k) % NY, (c + dc) % NC)
            to(tok.at[:, pl.ds(pl.multiple_of((d * 2 + i) * F, F), F)], tbuf.at[i * NF + mine], tsend.at[i], trecv.at[i * NF + mine], d, rep).start()
            return 0
        lax.fori_loop(max(q0 * L, 1), q1 * L, body, 0)

    def slot_dev(x, y, c):
        return x * (NY * NC) + y * NC + c

    own_g.wait()
    spread(y)

    def send_scale(k, _):
        to(sc.at[mine], sc.at[mine], ssem.at[0], rsem.at[0], (me + k) % NF, rep).start()
        return 0

    lax.fori_loop(1, NF, send_scale, 0)
    send_tokens(0, 0, NX)
    for t in range(1, NY):
        @pl.when(y >= t)
        def _():
            s = slot_of(x, y - t, c)
            wait(gbuf.at[s], grecv.at[s])
            spread(y - t)

        @pl.when(y + t < NY)
        def _():
            s = slot_of(x, y + t, c)
            wait(gbuf.at[s], grecv.at[s])
            spread(y + t)
    send_tokens(0, NX, NG)

    def take_grads(q):
        s0 = base_of(q)

        def body(j, _):
            s = s0 + j
            wait(gbuf.at[s], grecv.at[s])

            @pl.when(q < NX)
            def _():
                to(gbuf.at[s], gbuf.at[s], csend.at[s % (NX * NY)], grecv.at[s], me + 1 - 2 * c, rep).start()
            return 0
        lax.fori_loop(0, L, body, 0)

    def dnormed(q):
        s0 = base_of(q)
        r = lax.dot_general(gbuf[pl.ds(s0, L)].reshape(L * T, C), w[...], (((1,), (1,)), ((), ())), preferred_element_type=f32)
        dn[pl.ds(s0, L)] = r.reshape(L, T, 2 * F)

    def columns(ref):
        flat = jnp.concatenate([ref[s] for s in range(NF)] + [jnp.zeros((T - NF, T), f32)], axis=0).T
        return flat

    def gains(i):
        return gain[pl.ds(me * 2 + i, 1), :]

    def block(i, q):
        s0 = base_of(q)

        def arrive(j, _):
            wait(tbuf.at[i * NF + s0 + j], trecv.at[i * NF + s0 + j])
            return 0
        lax.fori_loop(0, L, arrive, 0)
        v = tbuf[pl.ds(i * NF + s0, L)].astype(f32)
        normed = (v * colc[0, pl.ds(s0, L)] * gains(i)).astype(bf16).reshape(L * T, F)
        part = lax.dot_general(normed, gbuf[pl.ds(s0, L)].reshape(L * T, C), (((0,), (0,)), ((), ())), preferred_element_type=f32)
        acc[i] += part
        return s0, v * gains(i) * dn[pl.ds(s0, L), :, i * F:(i + 1) * F]

    def first(q, _):
        @pl.when(q > 0)
        def _():
            take_grads(q)
        dnormed(q)
        s0, p = block(0, q)
        pacc[pl.ds(s0, L)] = p
        return 0

    acc[...] = jnp.zeros_like(acc)
    wait(sc.at[pl.ds(0, NF - 1)], rsem.at[0])
    flat = columns(sc)
    for s in range(NF):
        colc[0, s] = flat[:, s:s + 1]
    send_tokens(1, 0, NX)
    lax.fori_loop(0, NX, first, 0)
    send_tokens(1, NX, NG)
    lax.fori_loop(NX, NG, first, 0)

    def dw_scatter(i):
        if i:
            accb[...] = acc[i].astype(bf16)
        src, dst = (accb, rsb) if i else (acc.at[0], rsf)
        for p in range(OWN):
            zo = p // 2 * 3 + p % 2

            @pl.when(z != zo)
            def _():
                to(src.at[pl.ds(p * PR, PR)], dst.at[z], ssem.at[3 + i], rsem.at[3 + i], me, zo * NH + h).start()

    def dw_pair(i):
        dst = rsb if i else rsf

        @pl.when(owner)
        def _():
            wait(dst.at[pl.ds(0, NZ - 1)], rsem.at[3 + i])
            own = acc[i, pl.ds(pl.multiple_of(piece * PR, PR), PR)]
            dst[z] = jnp.zeros((PR, C), dst.dtype)
            psum[i] = functools.reduce(jnp.add, [own] + [dst[j].astype(f32) for j in range(NZ)])
            to(psum.at[i], prb.at[i], ssem.at[5 + i], rsem.at[5 + i], me, z * NH + 1 - h).start()

    def dw_gather(i):
        @pl.when(owner)
        def _():
            wait(prb.at[i], rsem.at[5 + i])
            agb[i, piece] = (psum[i] + prb[i]).astype(bf16)

            def body(k, _):
                to(agb.at[i, piece], agb.at[i, piece], ssem.at[7 + i], rsem.at[7 + i], me, (z + k) % NZ * NH + h).start()
                return 0
            lax.fori_loop(1, NZ, body, 0)

    def dw_finish(i):
        @pl.when(owner)
        def _():
            wait(agb.at[i, pl.ds(0, OWN - 1)], rsem.at[7 + i])

        @pl.when(jnp.logical_not(owner))
        def _():
            wait(agb.at[i, pl.ds(0, OWN)], rsem.at[7 + i])
        for p in range(OWN):
            dwb[pl.ds(i * F + p * PR, PR), :] = agb[i, p].astype(f32)
        local(dwb.at[pl.ds(i * F, F)], dw.at[pl.ds(i * F, F)], lsem.at[2 + i]).start()

    def second(q, _):
        s0, p = block(1, q)
        dx, dc = shift(q)
        p = p + pacc[pl.ds(s0, L)]
        for j in range(L):
            rows[0, s0 + j] = jnp.sum(p[j].T, axis=0, keepdims=True)
            d = slot_dev((x + NX - dx) % NX, j, (c + dc) % NC)

            @pl.when(d != me)
            def _():
                to(rows.at[0, s0 + j], rows.at[1, mine], ssem.at[1], rsem.at[1], d, rep).start()
        return 0

    dw_scatter(0)
    lax.fori_loop(0, NG, second, 0)
    dw_pair(0)
    dw_scatter(1)

    wait(rows.at[1, pl.ds(0, NF - 1)], rsem.at[1])
    rows[1, mine] = rows[0, mine]
    inner = functools.reduce(jnp.add, [rows[1, s] for s in range(NF)])
    srow = sc[mine]
    rows[2, mine] = srow * srow * srow * inner / D

    def send_coef(k, _):
        to(rows.at[2, mine], rows.at[2, mine], ssem.at[2], rsem.at[2], (me + k) % NF, rep).start()
        return 0

    lax.fori_loop(1, NF, send_coef, 0)
    dw_gather(0)
    dw_pair(1)
    wait(rows.at[2, pl.ds(0, NF - 1)], rsem.at[2])
    flat = columns(rows.at[2])
    for s in range(NF):
        colc[1, s] = flat[:, s:s + 1]

    dw_gather(1)

    def finish(k, _):
        xs = k // (NY * NC)
        s = slot_of(xs, (k // NC) % NY, k % NC)
        for i in range(2):
            a = colc[0, s] * gains(i) * dn[s, :, i * F:(i + 1) * F]
            dtb[k, :, i * F:(i + 1) * F] = (a - tbuf[i * NF + s].astype(f32) * colc[1, s]).astype(bf16)
        local(dtb.at[k], dt.at[pl.ds(pl.multiple_of(k * T, T), T)], lsem.at[4]).start()
        return 0

    lax.fori_loop(0, NF, finish, 0)
    dw_finish(0)
    dw_finish(1)

    for i in range(2):
        wait(tbuf.at[pl.ds(0, NF - 1)], tsend.at[i])
        wait(dwb.at[pl.ds(i * F, F)], lsem.at[2 + i])

        @pl.when(owner)
        def _():
            wait((accb if i else acc.at[0]).at[pl.ds(0, F - PR)], ssem.at[3 + i])
            wait(psum.at[i], ssem.at[5 + i])
            wait(agb.at[pl.ds(0, 1)].at[0, pl.ds(0, OWN)], ssem.at[7 + i])
            wait(agb.at[0, pl.ds(0, NZ - 1 - OWN)], ssem.at[7 + i])

        @pl.when(jnp.logical_not(owner))
        def _():
            wait(accb if i else acc.at[0], ssem.at[3 + i])
    for i in range(3):
        wait(rows.at[0, pl.ds(0, NF - 1)], ssem.at[i])
    for yy in range(NY):
        @pl.when(jnp.logical_and(yy <= y, y < NY - 1))
        def _():
            wait(gbuf.at[0], gsend.at[yy * 8])

        @pl.when(jnp.logical_and(yy >= y, y > 0))
        def _():
            wait(gbuf.at[0], gsend.at[yy * 8 + 1])
        for j in range(2, 6):
            wait(gbuf.at[0], gsend.at[yy * 8 + j])
    for q in range(1, NX):
        for j in range(L):
            wait(gbuf.at[0], csend.at[base_of(q) % (NX * NY) + j])
    wait(dtb, lsem.at[4])


def body(tokens, norm_gain, w_value, grad_value):
    hbm, anyspace, vmem = pl.BlockSpec(memory_space=pltpu.HBM), pl.BlockSpec(memory_space=pl.ANY), pl.BlockSpec(memory_space=pltpu.VMEM)
    dma = pltpu.SemaphoreType.DMA
    dw, dt = pl.pallas_call(
        kernel,
        out_shape=(jax.ShapeDtypeStruct((2 * F, C), f32), jax.ShapeDtypeStruct((NF * T, 2 * F), bf16)),
        in_specs=[hbm, vmem, vmem, hbm],
        out_specs=(anyspace, anyspace),
        scratch_shapes=[
            pltpu.VMEM((T, D), bf16),
            pltpu.VMEM((2 * NF, T, F), bf16),
            pltpu.VMEM((NF, T, C), bf16),
            pltpu.VMEM((NF, T, 2 * F), f32),
            pltpu.VMEM((NF, T, F), f32),
            pltpu.VMEM((NF, 1, T), f32),
            pltpu.VMEM((2, NF, T, 1), f32),
            pltpu.VMEM((3, NF, 1, T), f32),
            pltpu.VMEM((2, F, C), f32),
            pltpu.VMEM((F, C), bf16),
            pltpu.VMEM((NZ, PR, C), f32),
            pltpu.VMEM((NZ, PR, C), bf16),
            pltpu.VMEM((2, PR, C), f32),
            pltpu.VMEM((2, PR, C), f32),
            pltpu.VMEM((2, OWN, PR, C), bf16),
            pltpu.VMEM((NF, T, 2 * F), bf16),
            pltpu.VMEM((2 * F, C), f32),
            dma((5,)), dma((NY * 8,)), dma((NX * NY,)), dma((NF,)), dma((2,)), dma((2 * NF,)), dma((9,)), dma((9,)),
        ],
        compiler_params=pltpu.CompilerParams(collective_id=0, has_side_effects=True, vmem_limit_bytes=59 << 20),
    )(tokens.reshape(T, D), norm_gain.reshape(2 * NF, F), w_value, grad_value.reshape(T, C))
    return dw, dt.reshape(NF * T, 1, 2 * F)


def solution(mesh):
    assert mesh.shape["fsdp"] == NF and mesh.shape["rep"] == NR
    in_specs = (P("fsdp", "rep", None), P(), P("fsdp", None), P("fsdp", "rep", None))
    out_specs = (P("fsdp", None), P(None, "rep", "fsdp"))
    return jax.shard_map(body, mesh=mesh, in_specs=in_specs, out_specs=out_specs, check_vma=False)
```

```python
import functools
import jax
import jax.numpy as jnp
from jax import lax
from jax.experimental import pallas as pl
from jax.experimental.pallas import tpu as pltpu
from jax.sharding import PartitionSpec as P

MESH = pl.DeviceIdType.MESH
NX, NY, NC = 4, 4, 2
NZ, NH = 12, 2
NF, NR = NX * NY * NC, NZ * NH
T = 128
F = 128
C = 512
D = 2 * F * NF
OWN = 8
PR = F // OWN
L = NY
NG = NF // L
f32, bf16 = jnp.float32, jnp.bfloat16


def kernel(tok, gain_in, w_in, grd, dw, dt, vtok, tbuf, gbuf, dn, pacc, sc, colc, rows, acc, accb, rsb, psum, prb, agb, dtb, dwb, gain, w,
           lsem, gsend, csend, grecv, tsend, trecv, ssem, rsem):
    me, rep = lax.axis_index("fsdp"), lax.axis_index("rep")
    x, y, c = me // (NY * NC), (me // NC) % NY, me % NC
    z, h = rep // NH, rep % NH

    def slot_of(x, y, c):
        return c * (NX * NY) + x * NY + y

    def shift(q):
        r = q % NX
        return r + r // 2 * (1 - 2 * (r % 2)), q // NX

    def base_of(q):
        dx, dc = shift(q)
        return slot_of((x + NX - dx) % NX, 0, (c + dc) % NC)

    mine = slot_of(x, y, c)
    owner = z % 3 < 2
    piece = (z // 3) * 2 + z % 3

    def local(src, dst, sem):
        return pltpu.make_async_copy(src, dst, sem)

    def to(src, dst, ss, rs, f, r):
        return pltpu.make_async_remote_copy(src_ref=src, dst_ref=dst, send_sem=ss, recv_sem=rs, device_id=(f, r), device_id_type=MESH)

    def wait(ref, sem):
        pltpu.make_async_copy(ref, ref, sem).wait()

    bar = pltpu.get_barrier_semaphore()

    def greet_f(k, _):
        pl.semaphore_signal(bar, inc=1, device_id=((me + k) % NF, rep), device_id_type=MESH)
        return 0

    def greet_z(k, _):
        pl.semaphore_signal(bar, inc=1, device_id=(me, (z + k) % NZ * NH + h), device_id_type=MESH)
        return 0

    lax.fori_loop(1, NF, greet_f, 0)
    lax.fori_loop(1, NZ, greet_z, 0)
    pl.semaphore_signal(bar, inc=1, device_id=(me, z * NH + 1 - h), device_id_type=MESH)

    load = local(tok, vtok, lsem.at[0])
    load.start()
    own_g = local(grd, gbuf.at[mine], lsem.at[1])
    own_g.start()
    extra = [local(gain_in, gain, lsem.at[5]), local(w_in, w, lsem.at[6])]
    for cp in extra:
        cp.start()
    own_t = [local(tok.at[:, pl.ds(pl.multiple_of((me * 2 + i) * F, F), F)], tbuf.at[i * NF + mine], trecv.at[i * NF + mine]) for i in range(2)]
    for cp in own_t:
        cp.start()
    pl.semaphore_wait(bar, NF - 1 + NZ)

    def spread(yy):
        s = slot_of(x, yy, c)
        src = gbuf.at[s]

        @pl.when(jnp.logical_and(yy <= y, y < NY - 1))
        def _():
            to(src, src, gsend.at[yy * 8], grecv.at[s], me + NC, rep).start()

        @pl.when(jnp.logical_and(yy >= y, y > 0))
        def _():
            to(src, src, gsend.at[yy * 8 + 1], grecv.at[s], me - NC, rep).start()
        for j in range(1, NX):
            to(src, src, gsend.at[yy * 8 + 1 + j], grecv.at[s], (x + j) % NX * (NY * NC) + y * NC + c, rep).start()
        to(src, src, gsend.at[yy * 8 + 5], grecv.at[s], me + 1 - 2 * c, rep).start()

    def send_tokens(i, q0, q1):
        def body(k, _):
            dx, dc = shift(k // L)
            d = slot_dev((x + dx) % NX, (y + k) % NY, (c + dc) % NC)
            to(tok.at[:, pl.ds(pl.multiple_of((d * 2 + i) * F, F), F)], tbuf.at[i * NF + mine], tsend.at[i], trecv.at[i * NF + mine], d, rep).start()
            return 0
        lax.fori_loop(max(q0 * L, 1), q1 * L, body, 0)

    def slot_dev(x, y, c):
        return x * (NY * NC) + y * NC + c

    own_g.wait()
    spread(y)
    send_tokens(0, 0, NX)
    load.wait()

    def square(i, a):
        v = vtok[:, pl.ds(pl.multiple_of(i * F, F), F)].astype(f32)
        return a + v * v

    total = lax.fori_loop(0, D // F, square, jnp.zeros((T, F), f32), unroll=4)
    srow = lax.rsqrt(jnp.sum(total.T, axis=0, keepdims=True) / D + 1e-05)
    sc[mine] = srow

    def send_scale(k, _):
        to(sc.at[mine], sc.at[mine], ssem.at[0], rsem.at[0], (me + k) % NF, rep).start()
        return 0

    lax.fori_loop(1, NF, send_scale, 0)
    for t in range(1, NY):
        @pl.when(y >= t)
        def _():
            s = slot_of(x, y - t, c)
            wait(gbuf.at[s], grecv.at[s])
            spread(y - t)

        @pl.when(y + t < NY)
        def _():
            s = slot_of(x, y + t, c)
            wait(gbuf.at[s], grecv.at[s])
            spread(y + t)
    send_tokens(0, NX, NG)

    def take_grads(q):
        s0 = base_of(q)

        def body(j, _):
            s = s0 + j
            wait(gbuf.at[s], grecv.at[s])

            @pl.when(q < NX)
            def _():
                to(gbuf.at[s], gbuf.at[s], csend.at[s % (NX * NY)], grecv.at[s], me + 1 - 2 * c, rep).start()
            return 0
        lax.fori_loop(0, L, body, 0)

    def dnormed(q):
        s0 = base_of(q)
        r = lax.dot_general(gbuf[pl.ds(s0, L)].reshape(L * T, C), w[...], (((1,), (1,)), ((), ())), preferred_element_type=f32)
        dn[pl.ds(s0, L)] = r.reshape(L, T, 2 * F)

    def columns(ref):
        flat = jnp.concatenate([ref[s] for s in range(NF)] + [jnp.zeros((T - NF, T), f32)], axis=0).T
        return flat

    def gains(i):
        return gain[pl.ds(me * 2 + i, 1), :]

    def block(i, q):
        s0 = base_of(q)

        def arrive(j, _):
            wait(tbuf.at[i * NF + s0 + j], trecv.at[i * NF + s0 + j])
            return 0
        lax.fori_loop(0, L, arrive, 0)
        v = tbuf[pl.ds(i * NF + s0, L)].astype(f32)
        normed = (v * colc[0, pl.ds(s0, L)] * gains(i)).astype(bf16).reshape(L * T, F)
        part = lax.dot_general(normed, gbuf[pl.ds(s0, L)].reshape(L * T, C), (((0,), (0,)), ((), ())), preferred_element_type=f32)
        acc[i] += part
        return s0, v * gains(i) * dn[pl.ds(s0, L), :, i * F:(i + 1) * F]

    def first(q, _):
        @pl.when(q > 0)
        def _():
            take_grads(q)
        dnormed(q)
        s0, p = block(0, q)
        pacc[pl.ds(s0, L)] = p
        return 0

    for cp in extra:
        cp.wait()
    acc[...] = jnp.zeros_like(acc)
    wait(sc.at[pl.ds(0, NF - 1)], rsem.at[0])
    flat = columns(sc)
    for s in range(NF):
        colc[0, s] = flat[:, s:s + 1]
    send_tokens(1, 0, NX)
    lax.fori_loop(0, NX, first, 0)
    send_tokens(1, NX, NG)
    lax.fori_loop(NX, NG, first, 0)

    def dw_scatter(i):
        accb[i] = acc[i].astype(bf16)
        src, dst = accb.at[i], rsb.at[i]
        for p in range(OWN):
            zo = p // 2 * 3 + p % 2

            @pl.when(z != zo)
            def _():
                to(src.at[pl.ds(p * PR, PR)], dst.at[z], ssem.at[3 + i], rsem.at[3 + i], me, zo * NH + h).start()

    def dw_pair(i):
        dst = rsb.at[i]

        @pl.when(owner)
        def _():
            wait(dst.at[pl.ds(0, NZ - 1)], rsem.at[3 + i])
            own = acc[i, pl.ds(pl.multiple_of(piece * PR, PR), PR)]
            dst[z] = jnp.zeros((PR, C), dst.dtype)
            psum[i] = functools.reduce(jnp.add, [own] + [dst[j].astype(f32) for j in range(NZ)])
            to(psum.at[i], prb.at[i], ssem.at[5 + i], rsem.at[5 + i], me, z * NH + 1 - h).start()

    def dw_gather(i):
        @pl.when(owner)
        def _():
            wait(prb.at[i], rsem.at[5 + i])
            agb[i, piece] = (psum[i] + prb[i]).astype(bf16)

            def body(k, _):
                to(agb.at[i, piece], agb.at[i, piece], ssem.at[7 + i], rsem.at[7 + i], me, (z + k) % NZ * NH + h).start()
                return 0
            lax.fori_loop(1, NZ, body, 0)

    def dw_finish(i):
        @pl.when(owner)
        def _():
            wait(agb.at[i, pl.ds(0, OWN - 1)], rsem.at[7 + i])

        @pl.when(jnp.logical_not(owner))
        def _():
            wait(agb.at[i, pl.ds(0, OWN)], rsem.at[7 + i])
        for p in range(OWN):
            dwb[pl.ds(i * F + p * PR, PR), :] = agb[i, p].astype(f32)
        local(dwb.at[pl.ds(i * F, F)], dw.at[pl.ds(i * F, F)], lsem.at[2 + i]).start()

    def second(q, _):
        s0, p = block(1, q)
        dx, dc = shift(q)
        p = p + pacc[pl.ds(s0, L)]
        for i in range(2):
            cols = slice(i * F, (i + 1) * F)
            dn[pl.ds(s0, L), :, cols] = colc[0, pl.ds(s0, L)] * gains(i) * dn[pl.ds(s0, L), :, cols]
        for j in range(L):
            rows[0, s0 + j] = jnp.sum(p[j].T, axis=0, keepdims=True)
            d = slot_dev((x + NX - dx) % NX, j, (c + dc) % NC)

            @pl.when(d != me)
            def _():
                to(rows.at[0, s0 + j], rows.at[1, mine], ssem.at[1], rsem.at[1], d, rep).start()
        return 0

    dw_scatter(0)
    lax.fori_loop(0, NG - 1, second, 0)
    dw_pair(0)
    lax.fori_loop(NG - 1, NG, second, 0)
    dw_scatter(1)

    wait(rows.at[1, pl.ds(0, NF - 1)], rsem.at[1])
    rows[1, mine] = rows[0, mine]
    inner = functools.reduce(jnp.add, [rows[1, s] for s in range(NF)])
    srow = sc[mine]
    rows[2, mine] = srow * srow * srow * inner / D

    def send_coef(k, _):
        to(rows.at[2, mine], rows.at[2, mine], ssem.at[2], rsem.at[2], (me + k) % NF, rep).start()
        return 0

    lax.fori_loop(1, NF, send_coef, 0)
    dw_gather(0)
    dw_pair(1)
    wait(rows.at[2, pl.ds(0, NF - 1)], rsem.at[2])
    flat = columns(rows.at[2])
    for s in range(NF):
        colc[1, s] = flat[:, s:s + 1]

    dw_gather(1)

    def finish(k, _):
        xs = k // (NY * NC)
        s = slot_of(xs, (k // NC) % NY, k % NC)
        coef = colc[1, s]
        for i in range(2):
            dtb[k, :, i * F:(i + 1) * F] = (dn[s, :, i * F:(i + 1) * F] - tbuf[i * NF + s].astype(f32) * coef).astype(bf16)
        local(dtb.at[k], dt.at[pl.ds(pl.multiple_of(k * T, T), T)], lsem.at[4]).start()
        return 0

    lax.fori_loop(0, NF, finish, 0)
    dw_finish(0)
    dw_finish(1)

    for i in range(2):
        wait(tbuf.at[pl.ds(0, NF - 1)], tsend.at[i])
        wait(dwb.at[pl.ds(i * F, F)], lsem.at[2 + i])

        @pl.when(owner)
        def _():
            wait(accb.at[i, pl.ds(0, F - PR)], ssem.at[3 + i])
            wait(psum.at[i], ssem.at[5 + i])
            wait(agb.at[pl.ds(0, 1)].at[0, pl.ds(0, OWN)], ssem.at[7 + i])
            wait(agb.at[0, pl.ds(0, NZ - 1 - OWN)], ssem.at[7 + i])

        @pl.when(jnp.logical_not(owner))
        def _():
            wait(accb.at[i], ssem.at[3 + i])
    for i in range(3):
        wait(rows.at[0, pl.ds(0, NF - 1)], ssem.at[i])
    for yy in range(NY):
        @pl.when(jnp.logical_and(yy <= y, y < NY - 1))
        def _():
            wait(gbuf.at[0], gsend.at[yy * 8])

        @pl.when(jnp.logical_and(yy >= y, y > 0))
        def _():
            wait(gbuf.at[0], gsend.at[yy * 8 + 1])
        for j in range(2, 6):
            wait(gbuf.at[0], gsend.at[yy * 8 + j])
    for q in range(1, NX):
        for j in range(L):
            wait(gbuf.at[0], csend.at[base_of(q) % (NX * NY) + j])
    wait(dtb, lsem.at[4])


def body(tokens, norm_gain, w_value, grad_value):
    hbm, anyspace = pl.BlockSpec(memory_space=pltpu.HBM), pl.BlockSpec(memory_space=pl.ANY)
    dma = pltpu.SemaphoreType.DMA
    dw, dt = pl.pallas_call(
        kernel,
        out_shape=(jax.ShapeDtypeStruct((2 * F, C), f32), jax.ShapeDtypeStruct((NF * T, 2 * F), bf16)),
        in_specs=[hbm] * 4,
        out_specs=(anyspace, anyspace),
        scratch_shapes=[
            pltpu.VMEM((T, D), bf16),
            pltpu.VMEM((2 * NF, T, F), bf16),
            pltpu.VMEM((NF, T, C), bf16),
            pltpu.VMEM((NF, T, 2 * F), f32),
            pltpu.VMEM((NF, T, F), f32),
            pltpu.VMEM((NF, 1, T), f32),
            pltpu.VMEM((2, NF, T, 1), f32),
            pltpu.VMEM((3, NF, 1, T), f32),
            pltpu.VMEM((2, F, C), f32),
            pltpu.VMEM((2, F, C), bf16),
            pltpu.VMEM((2, NZ, PR, C), bf16),
            pltpu.VMEM((2, PR, C), f32),
            pltpu.VMEM((2, PR, C), f32),
            pltpu.VMEM((2, OWN, PR, C), bf16),
            pltpu.VMEM((NF, T, 2 * F), bf16),
            pltpu.VMEM((2 * F, C), f32),
            pltpu.VMEM((2 * NF, F), f32),
            pltpu.VMEM((2 * F, C), bf16),
            dma((7,)), dma((NY * 8,)), dma((NX * NY,)), dma((NF,)), dma((2,)), dma((2 * NF,)), dma((9,)), dma((9,)),
        ],
        compiler_params=pltpu.CompilerParams(collective_id=0, has_side_effects=True, vmem_limit_bytes=59 << 20),
    )(tokens.reshape(T, D), norm_gain.reshape(2 * NF, F), w_value, grad_value.reshape(T, C))
    return dw, dt.reshape(NF * T, 1, 2 * F)


def solution(mesh):
    assert mesh.shape["fsdp"] == NF and mesh.shape["rep"] == NR
    in_specs = (P("fsdp", "rep", None), P(), P("fsdp", None), P("fsdp", "rep", None))
    out_specs = (P("fsdp", None), P(None, "rep", "fsdp"))
    return jax.shard_map(body, mesh=mesh, in_specs=in_specs, out_specs=out_specs, check_vma=False)
```
